32 devices in a mesh: groups: 2 (over y), gx: 2 (over core), gy: 8 (over z, x).
Axes of the slice: x: 2, y: 2, z: 4, core: 2. Of those that a mesh axis runs over, the one named last changes fastest.
Arguments:
- tokens: bfloat16 [512, 8192], P(('groups', 'gy'), 'gx'), parts along dimension 0, may hold values from -6 to 6
- gate_weight: bfloat16 [8192, 26624], P('gx', 'gy'), may hold values from -0.0625 to 0.0625
- up_weight: bfloat16 [8192, 26624], P('gx', 'gy'), may hold values from -0.0625 to 0.0625
- down_weight: bfloat16 [26624, 8192], P('gy', 'gx'), may hold values from -0.0546875 to 0.0546875
Outputs:
- mixed: bfloat16 [512, 8192], P(('groups', 'gy'), 'gx'), parts along dimension 0
The draws below stay inside these ranges and needn't reach their ends.
There are 2 independent parts, one for each index of `groups`. The reference program is written for one: setup_inputs(seed, part) draws one part's arguments, and reference() takes and returns one part's arrays. A program takes and returns all parts, laid end to end along the dimension named above; an argument that names none is the same for every part. Nothing has to cross between parts.
All inputs are finite; a program needn't handle non-finite values.
Results may differ from the reference program's by a relative error of at most 0.0049.
Values may be sent and summed in bfloat16 or wider, within the bound.
A program may use at most 192 MiB of HBM per device.

```python
import jax
import jax.numpy as jnp

D = 8192
FF = 26624
TOKENS = 256


def spiked(drawn, key, source, target, parts, factor):
    def block_of(dim):
        return (jnp.arange(drawn.shape[dim]) // (drawn.shape[dim] // parts)).reshape((-1,) + (1,) * (drawn.ndim - 1 - dim))

    near = jax.random.permutation(key, parts)[block_of(target)]
    second = (block_of(target) + parts // 2) % parts
    return jnp.where((block_of(source) == near) | (block_of(source) == second), factor * drawn, drawn)


def block_levels(own_key, dims, split, smallest, largest):
    level, own = 1.0, jax.random.fold_in(own_key, 6)
    for dim, parts in split:
        heights = jnp.exp(jax.random.uniform(jax.random.fold_in(own, dim), (parts,), jnp.float32, smallest / len(split), largest / len(split)))
        level = level * jnp.repeat(heights, dims[dim] // parts).reshape([-1 if axis == dim else 1 for axis in range(len(dims))])
    return level


def centred(key, shape, deviation, limit, pieces=(), dtype=jnp.bfloat16):
    factor_of = block_levels(key, shape, pieces, -0.22, 0.18) if pieces else 1.0
    entries = jax.random.normal(key, shape, jnp.float32) * deviation * factor_of
    return jnp.minimum(jnp.maximum(entries, -limit), limit).astype(dtype)


def bell_draw_with(own_key, dims, scale, bound, split, heavy, held_as=jnp.bfloat16):
    drawn = scale * jax.random.normal(own_key, dims, jnp.float32)
    if split:
        drawn = drawn * block_levels(own_key, dims, split, -0.22, 0.18)
    return jnp.clip(spiked(drawn, jax.random.fold_in(own_key, 3), *heavy), -bound, bound).astype(held_as)


def setup_inputs(seed: int = 0, part: int = 0) -> dict:
    arg_keys = jax.random.split(jax.random.key(seed), 5)
    part_splits = jax.random.split(jax.random.fold_in(arg_keys[4], part), 5)
    tokens = centred(part_splits[0], (TOKENS, D), 1.0, 6.0, ((0, 8), (1, 2)))
    gate_weight = centred(arg_keys[1], (D, FF), D ** -0.5, 0.0625, ((0, 2), (1, 8)))
    up_weight = centred(arg_keys[2], (D, FF), D ** -0.5, 0.0625, ((0, 2), (1, 8)))
    down_weight = bell_draw_with(arg_keys[3], (FF, D), FF ** -0.5, 0.0546875, ((0, 8), (1, 2)), (0, 1, 8, 2.0))
    return dict(tokens=tokens, gate_weight=gate_weight, up_weight=up_weight, down_weight=down_weight)


def reference(tokens, gate_weight, up_weight, down_weight):
    gate = jnp.dot(tokens, gate_weight, preferred_element_type=jnp.float32)
    up = jnp.dot(tokens, up_weight, preferred_element_type=jnp.float32)
    hidden = (jax.nn.silu(gate) * up).astype(jnp.bfloat16)
    return jnp.dot(hidden, down_weight, preferred_element_type=jnp.float32).astype(jnp.bfloat16)
```

```python
import functools

import jax
import jax.numpy as jnp
from jax import lax
from jax.experimental import pallas as pl
from jax.experimental.pallas import tpu as pltpu
from jax.sharding import PartitionSpec as P

F32, BF16 = jnp.float32, jnp.bfloat16
MESH = pl.DeviceIdType.MESH
CW = 256
RING = 10
KEEP = 4
LAG = 2
CUT = 2
EX = F32


def local(tokens, gate_weight, up_weight, down_weight):
    piece = lax.all_gather(tokens, "gy", axis=0, tiled=True)
    gate_part = jnp.dot(piece, gate_weight, preferred_element_type=F32)
    up_part = jnp.dot(piece, up_weight, preferred_element_type=F32)
    gate, up = lax.psum((gate_part, up_part), "gx")
    hidden = (jax.nn.silu(gate) * up).astype(BF16)
    summed = lax.psum_scatter(
        jnp.dot(hidden, down_weight, preferred_element_type=F32), "gy", scatter_dimension=0, tiled=True
    )
    return summed.astype(BF16)


def kernel(rows, width, units, nz,
           tok, gw, uw, dw, out,
           ring, x_all, hid, part, precv, yown, xsend, xrecv, zsend, zrecv, fin,
           ring_sem, own_sem, up_send, dn_send, line_recv, xf_send, xf_recv,
           part_send, part_recv, hid_send, hid_recv, xs_send, xs_recv, zs_send, zs_recv):
    gx = lax.axis_index("gx")
    gy = lax.axis_index("gy")
    z, x = gy // 2, gy % 2
    line = nz * rows
    half = line
    chunks, groups = units // CW, width // (2 * CW)
    core = {"gx": 1 - gx}
    across = {"gy": z * 2 + 1 - x}

    def along(zz):
        return {"gy": zz * 2 + x}

    def gu_copy(c, which):
        src = (gw, uw)[which].at[:, pl.ds(pl.multiple_of(c * CW, CW), CW)]
        s = c % RING
        return pltpu.make_async_copy(src, ring.at[s, which], ring_sem.at[s, which])

    def d_copy(g, which):
        src = dw.at[:, pl.ds(pl.multiple_of((g * 2 + which) * CW, CW), CW)]
        s = (chunks + g) % RING
        return pltpu.make_async_copy(src, ring.at[s, which, pl.ds(0, units)], ring_sem.at[s, which])

    for c in range(min(RING, chunks)):
        gu_copy(c, 0).start()
        gu_copy(c, 1).start()

    barrier = pltpu.get_barrier_semaphore()
    pl.semaphore_signal(barrier, inc=1, device_id=core, device_id_type=MESH)
    pl.semaphore_signal(barrier, inc=1, device_id=across, device_id_type=MESH)
    for k in range(1, nz):
        pl.semaphore_signal(barrier, inc=1, device_id=along(lax.rem(z + k, nz)), device_id_type=MESH)
    pl.semaphore_wait(barrier, nz + 1)

    cut = rows // CUT

    def place(block, h, far):
        return x_all.at[pl.ds(pl.multiple_of(far * line + block * rows + h * cut, cut), cut)]

    def source(block, h, own):
        return tok.at[pl.ds(h * cut, cut)] if own else place(block, h, 0)

    def line_copy(block, h, own, step, sems):
        return pltpu.make_async_remote_copy(
            src_ref=source(block, h, own), dst_ref=place(block, h, 0),
            send_sem=sems.at[block, h], recv_sem=line_recv.at[block, h],
            device_id=along(z + step), device_id_type=MESH)

    def cross_copy(block, h, own):
        return pltpu.make_async_remote_copy(
            src_ref=source(block, h, own), dst_ref=place(block, h, 1),
            send_sem=xf_send.at[block, h], recv_sem=xf_recv.at[block, h],
            device_id=across, device_id_type=MESH)

    for h in range(CUT):
        @pl.when(z < nz - 1)
        def _():
            line_copy(z, h, True, 1, up_send).start()

        @pl.when(z > 0)
        def _():
            line_copy(z, h, True, -1, dn_send).start()

        cross_copy(z, h, True).start()
    keep = pltpu.make_async_copy(tok, x_all.at[pl.ds(pl.multiple_of(z * rows, rows), rows)], own_sem)
    keep.start()
    for t in range(1, nz):
        for h in range(CUT):
            @pl.when(z - t >= 0)
            def _():
                line_copy(z - t, h, False, 1, up_send).wait_recv()

                @pl.when(z < nz - 1)
                def _():
                    line_copy(z - t, h, False, 1, up_send).start()

                cross_copy(z - t, h, False).start()

            @pl.when(z + t < nz)
            def _():
                line_copy(z + t, h, False, -1, dn_send).wait_recv()

                @pl.when(z > 0)
                def _():
                    line_copy(z + t, h, False, -1, dn_send).start()

                cross_copy(z + t, h, False).start()
    keep.wait()
    for b in range(nz):
        for h in range(CUT):
            cross_copy(b, h, False).wait_recv()

    def part_copy(c):
        return pltpu.make_async_remote_copy(
            src_ref=part.at[c % KEEP, 1 - gx], dst_ref=precv.at[c],
            send_sem=part_send.at[c % KEEP], recv_sem=part_recv.at[c],
            device_id=core, device_id_type=MESH)

    def hid_at(c, which):
        return hid.at[pl.ds(pl.multiple_of(which * half, half), half), pl.ds(pl.multiple_of(c * CW, CW), CW)]

    def hid_copy(c, which):
        return pltpu.make_async_remote_copy(
            src_ref=hid_at(c, which), dst_ref=hid_at(c, which),
            send_sem=hid_send.at[c], recv_sem=hid_recv.at[c],
            device_id=core, device_id_type=MESH)

    def finish(c):
        part_copy(c).wait_recv()
        gate = part[c % KEEP, gx, 0].astype(F32) + precv[c, 0].astype(F32)
        up = part[c % KEEP, gx, 1].astype(F32) + precv[c, 1].astype(F32)
        hid_at(c, gx)[...] = (gate / (1.0 + jnp.exp(-gate)) * up).astype(BF16)
        hid_copy(c, gx).start()

    def gu_step(c, carry):
        s = c % RING

        @pl.when(c >= KEEP)
        def _():
            part_copy(c - KEEP).wait_send()

        for which in range(2):
            gu_copy(c, which).wait()
            term = jnp.dot(x_all[...], ring[s, which], preferred_element_type=F32)
            part[c % KEEP, 0, which] = term[:half].astype(part.dtype)
            part[c % KEEP, 1, which] = term[half:].astype(part.dtype)
        part_copy(c).start()
        nxt = c + RING

        @pl.when(nxt < chunks)
        def _():
            gu_copy(nxt, 0).start()
            gu_copy(nxt, 1).start()

        @pl.when((nxt >= chunks) & (nxt < chunks + groups))
        def _():
            d_copy(nxt - chunks, 0).start()
            d_copy(nxt - chunks, 1).start()

        @pl.when(c >= 1)
        def _():
            finish(c - 1)
        return carry

    lax.fori_loop(0, chunks, gu_step, 0)
    finish(chunks - 1)
    for c in range(chunks):
        hid_copy(c, 1 - gx).wait_recv()

    def x_copy(g):
        return pltpu.make_async_remote_copy(
            src_ref=xsend.at[g], dst_ref=xrecv.at[g], send_sem=xs_send.at[g], recv_sem=xs_recv.at[g],
            device_id=across, device_id_type=MESH)

    def z_copy(g, k):
        return pltpu.make_async_remote_copy(
            src_ref=zsend.at[k - 1, g], dst_ref=zrecv.at[k - 1, g],
            send_sem=zs_send.at[k - 1, g], recv_sem=zs_recv.at[k - 1, g],
            device_id=along(lax.rem(z + k, nz)), device_id_type=MESH)

    def pair(g):
        x_copy(g).wait_recv()
        for k in range(nz):
            at = pl.ds(pl.multiple_of(lax.rem(z + k, nz) * rows, rows), rows)
            both = yown[g, :, at, :] + xrecv[g, :, at, :].astype(F32)
            if k == 0:
                fin[g] = both
            else:
                zsend[k - 1, g] = both.astype(BF16)
                z_copy(g, k).start()

    def d_step(g, carry):
        s = (chunks + g) % RING
        for which in range(2):
            d_copy(g, which).wait()
            y = jnp.dot(hid[...], ring[s, which, :units], preferred_element_type=F32)
            yown[g, which] = y[:line]
            xsend[g, which] = y[line:].astype(BF16)
        x_copy(g).start()

        @pl.when(g >= LAG)
        def _():
            pair(g - LAG)
        return carry

    lax.fori_loop(0, groups, d_step, 0)
    for g in range(groups - LAG, groups):
        pair(g)
    for g in range(groups):
        total = fin[g]
        for k in range(1, nz):
            z_copy(g, k).wait_recv()
            total = total + zrecv[k - 1, g].astype(F32)
        for which in range(2):
            out[:, pl.ds((g * 2 + which) * CW, CW)] = total[which].astype(BF16)

    for h in range(CUT):
        for b in range(nz):
            cross_copy(b, h, False).wait_send()

            @pl.when((z < nz - 1) & (b <= z))
            def _():
                line_copy(b, h, False, 1, up_send).wait_send()

            @pl.when((z > 0) & (b >= z))
            def _():
                line_copy(b, h, False, -1, dn_send).wait_send()
    for c in range(max(chunks - KEEP, 0), chunks):
        part_copy(c).wait_send()
    for c in range(chunks):
        hid_copy(c, gx).wait_send()
    for g in range(groups):
        x_copy(g).wait_send()
        for k in range(1, nz):
            z_copy(g, k).wait_send()


def fused(nz, tokens, gate_weight, up_weight, down_weight):
    rows, depth = tokens.shape
    units, width = down_weight.shape
    line = nz * rows
    chunks, groups = units // CW, width // (2 * CW)
    dma = pltpu.SemaphoreType.DMA
    flops = 2 * 2 * line * units * (2 * depth + width)
    return pl.pallas_call(
        functools.partial(kernel, rows, width, units, nz),
        out_shape=jax.ShapeDtypeStruct((rows, width), BF16),
        in_specs=[pl.BlockSpec(memory_space=pl.ANY)] * 4,
        out_specs=pl.BlockSpec(memory_space=pltpu.VMEM),
        scratch_shapes=[
            pltpu.VMEM((RING, 2, depth, CW), BF16),
            pltpu.VMEM((2 * line, depth), BF16),
            pltpu.VMEM((2 * line, units), BF16),
            pltpu.VMEM((KEEP, 2, 2, line, CW), EX),
            pltpu.VMEM((chunks, 2, line, CW), EX),
            pltpu.VMEM((groups, 2, line, CW), F32),
            pltpu.VMEM((groups, 2, line, CW), BF16),
            pltpu.VMEM((groups, 2, line, CW), BF16),
            pltpu.VMEM((nz - 1, groups, 2, rows, CW), BF16),
            pltpu.VMEM((nz - 1, groups, 2, rows, CW), BF16),
            pltpu.VMEM((groups, 2, rows, CW), F32),
            dma((RING, 2)),
            dma,
            dma((nz, CUT)),
            dma((nz, CUT)),
            dma((nz, CUT)),
            dma((nz, CUT)),
            dma((nz, CUT)),
            dma((KEEP,)),
            dma((chunks,)),
            dma((chunks,)),
            dma((chunks,)),
            dma((groups,)),
            dma((groups,)),
            dma((nz - 1, groups)),
            dma((nz - 1, groups)),
        ],
        compiler_params=pltpu.CompilerParams(
            collective_id=0, has_side_effects=True, vmem_limit_bytes=60 * 2**20
        ),
        cost_estimate=pl.CostEstimate(
            flops=flops, bytes_accessed=2 * units * (2 * depth + width), transcendentals=line * units
        ),
    )(tokens, gate_weight, up_weight, down_weight)


def solution(mesh):
    placed = (P(("groups", "gy"), "gx"), P("gx", "gy"), P("gx", "gy"), P("gy", "gx"))
    gy, gx = mesh.shape["gy"], mesh.shape["gx"]

    def run(tokens, gate_weight, up_weight, down_weight):
        rows, depth = tokens.shape
        units, width = down_weight.shape
        fits = gy == 8 and gx == 2 and rows == 32 and units % CW == 0 and width % (2 * CW) == 0
        fits = fits and units <= depth == width <= 4096
        fits = fits and RING >= width // (2 * CW) and units // CW >= KEEP
        fits = fits and RING <= units // CW and units <= 3328
        if fits:
            return fused(gy // 2, tokens, gate_weight, up_weight, down_weight)
        return local(tokens, gate_weight, up_weight, down_weight)

    return jax.shard_map(
        run, mesh=mesh, in_specs=placed, out_specs=P(("groups", "gy"), "gx"), check_vma=False
    )
```

```python
import functools

import jax
import jax.numpy as jnp
from jax import lax
from jax.experimental import pallas as pl
from jax.experimental.pallas import tpu as pltpu
from jax.sharding import PartitionSpec as P

F32, BF16 = jnp.float32, jnp.bfloat16
MESH = pl.DeviceIdType.MESH
CW = 256
RING = 10
KEEP = 4
LAG = 2
CUT = 2


def local(tokens, gate_weight, up_weight, down_weight):
    piece = lax.all_gather(tokens, "gy", axis=0, tiled=True)
    gate_part = jnp.dot(piece, gate_weight, preferred_element_type=F32)
    up_part = jnp.dot(piece, up_weight, preferred_element_type=F32)
    gate, up = lax.psum((gate_part, up_part), "gx")
    hidden = (jax.nn.silu(gate) * up).astype(BF16)
    summed = lax.psum_scatter(
        jnp.dot(hidden, down_weight, preferred_element_type=F32), "gy", scatter_dimension=0, tiled=True
    )
    return summed.astype(BF16)


def kernel(rows, width, units, nz,
           tok, gw, uw, dw, out,
           ring, x_all, hid, part, precv, yown, xsend, xrecv, zsend, zrecv, fin,
           ring_sem, own_sem, up_send, dn_send, line_recv, xf_send, xf_recv,
           part_send, part_recv, hid_send, hid_recv, xs_send, xs_recv, zs_send, zs_recv):
    gx = lax.axis_index("gx")
    gy = lax.axis_index("gy")
    z, x = gy // 2, gy % 2
    line = nz * rows
    half = line // 2
    chunks, groups = units // CW, width // (2 * CW)
    core = {"gx": 1 - gx}
    across = {"gy": z * 2 + 1 - x}

    def along(zz):
        return {"gy": zz * 2 + x}

    def gu_copy(c, which):
        src = (gw, uw)[which].at[:, pl.ds(pl.multiple_of(c * CW, CW), CW)]
        s = c % RING
        return pltpu.make_async_copy(src, ring.at[s, :, pl.ds(which * CW, CW)], ring_sem.at[s, which])

    def d_copy(g):
        src = dw.at[:, pl.ds(pl.multiple_of(g * 2 * CW, 2 * CW), 2 * CW)]
        s = (chunks + g) % RING
        return pltpu.make_async_copy(src, ring.at[s, pl.ds(0, units)], ring_sem.at[s, 0])

    for c in range(min(RING, chunks)):
        gu_copy(c, 0).start()
        gu_copy(c, 1).start()

    barrier = pltpu.get_barrier_semaphore()
    pl.semaphore_signal(barrier, inc=1, device_id=core, device_id_type=MESH)
    pl.semaphore_signal(barrier, inc=1, device_id=across, device_id_type=MESH)
    for k in range(1, nz):
        pl.semaphore_signal(barrier, inc=1, device_id=along(lax.rem(z + k, nz)), device_id_type=MESH)
    pl.semaphore_wait(barrier, nz + 1)

    cut = rows // CUT

    def place(block, h, far):
        return x_all.at[pl.ds(pl.multiple_of(far * line + block * rows + h * cut, cut), cut)]

    def source(block, h, own):
        return tok.at[pl.ds(h * cut, cut)] if own else place(block, h, 0)

    def line_copy(block, h, own, step, sems):
        return pltpu.make_async_remote_copy(
            src_ref=source(block, h, own), dst_ref=place(block, h, 0),
            send_sem=sems.at[block, h], recv_sem=line_recv.at[block, h],
            device_id=along(z + step), device_id_type=MESH)

    def cross_copy(block, h, own):
        return pltpu.make_async_remote_copy(
            src_ref=source(block, h, own), dst_ref=place(block, h, 1),
            send_sem=xf_send.at[block, h], recv_sem=xf_recv.at[block, h],
            device_id=across, device_id_type=MESH)

    for h in range(CUT):
        @pl.when(z < nz - 1)
        def _():
            line_copy(z, h, True, 1, up_send).start()

        @pl.when(z > 0)
        def _():
            line_copy(z, h, True, -1, dn_send).start()

        cross_copy(z, h, True).start()
    keep = pltpu.make_async_copy(tok, x_all.at[pl.ds(pl.multiple_of(z * rows, rows), rows)], own_sem)
    keep.start()
    for t in range(1, nz):
        for h in range(CUT):
            @pl.when(z - t >= 0)
            def _():
                line_copy(z - t, h, False, 1, up_send).wait_recv()

                @pl.when(z < nz - 1)
                def _():
                    line_copy(z - t, h, False, 1, up_send).start()

                cross_copy(z - t, h, False).start()

            @pl.when(z + t < nz)
            def _():
                line_copy(z + t, h, False, -1, dn_send).wait_recv()

                @pl.when(z > 0)
                def _():
                    line_copy(z + t, h, False, -1, dn_send).start()

                cross_copy(z + t, h, False).start()
    keep.wait()

    def part_copy(q):
        return pltpu.make_async_remote_copy(
            src_ref=part.at[q % KEEP, 1 - gx], dst_ref=precv.at[q],
            send_sem=part_send.at[q % KEEP], recv_sem=part_recv.at[q],
            device_id=core, device_id_type=MESH)

    def hid_at(far, c, which):
        at = pl.ds(pl.multiple_of(far * line + which * half, half), half)
        return hid.at[at, pl.ds(pl.multiple_of(c * CW, CW), CW)]

    def hid_copy(q, far, c, which):
        return pltpu.make_async_remote_copy(
            src_ref=hid_at(far, c, which), dst_ref=hid_at(far, c, which),
            send_sem=hid_send.at[q], recv_sem=hid_recv.at[q],
            device_id=core, device_id_type=MESH)

    def finish(q, far, c):
        part_copy(q).wait_recv()
        both = part[q % KEEP, gx] + precv[q]
        gate, up = both[:, :CW], both[:, CW:]
        hid_at(far, c, gx)[...] = (gate / (1.0 + jnp.exp(-gate)) * up).astype(BF16)
        hid_copy(q, far, c, gx).start()

    def multiply(q, far, c):
        @pl.when(q >= KEEP)
        def _():
            part_copy(q - KEEP).wait_send()

        term = jnp.dot(x_all[far * line:(far + 1) * line], ring[c % RING], preferred_element_type=F32)
        part[q % KEEP, 0] = term[:half]
        part[q % KEEP, 1] = term[half:]
        part_copy(q).start()

    def arrive(c):
        gu_copy(c, 0).wait()
        gu_copy(c, 1).wait()

    def refill(c):
        nxt = c + RING

        @pl.when(nxt < chunks)
        def _():
            gu_copy(nxt, 0).start()
            gu_copy(nxt, 1).start()

        @pl.when((nxt >= chunks) & (nxt < chunks + groups))
        def _():
            d_copy(nxt - chunks).start()

    def near_step(c, carry):
        arrive(c)
        multiply(c, 0, c)

        @pl.when(c >= 1)
        def _():
            finish(c - 1, 0, c - 1)
        return carry

    def far_step(c, carry):
        q = RING + c
        multiply(q, 1, c)
        refill(c)

        @pl.when(c == 0)
        def _():
            finish(RING - 1, 0, RING - 1)

        @pl.when(c >= 1)
        def _():
            finish(q - 1, 1, c - 1)
        return carry

    def both_step(c, carry):
        q = 2 * c
        arrive(c)
        multiply(q, 0, c)
        finish(q - 1, 1, c - 1)
        multiply(q + 1, 1, c)
        refill(c)
        finish(q, 0, c)
        return carry

    lax.fori_loop(0, RING, near_step, 0)
    for b in range(nz):
        for h in range(CUT):
            cross_copy(b, h, False).wait_recv()
    lax.fori_loop(0, RING, far_step, 0)
    lax.fori_loop(RING, chunks, both_step, 0)
    finish(2 * chunks - 1, 1, chunks - 1)
    order = [(0, c) for c in range(RING)] + [(1, c) for c in range(RING)]
    order += [(far, c) for c in range(RING, chunks) for far in range(2)]
    for q, (far, c) in enumerate(order):
        hid_copy(q, far, c, 1 - gx).wait_recv()

    def x_copy(g):
        return pltpu.make_async_remote_copy(
            src_ref=xsend.at[g], dst_ref=xrecv.at[g], send_sem=xs_send.at[g], recv_sem=xs_recv.at[g],
            device_id=across, device_id_type=MESH)

    def z_copy(g, k):
        return pltpu.make_async_remote_copy(
            src_ref=zsend.at[k - 1, g], dst_ref=zrecv.at[k - 1, g],
            send_sem=zs_send.at[k - 1, g], recv_sem=zs_recv.at[k - 1, g],
            device_id=along(lax.rem(z + k, nz)), device_id_type=MESH)

    def pair(g):
        x_copy(g).wait_recv()
        for k in range(nz):
            at = pl.ds(pl.multiple_of(lax.rem(z + k, nz) * rows, rows), rows)
            both = yown[g, at] + xrecv[g, at].astype(F32)
            if k == 0:
                fin[g] = both
            else:
                zsend[k - 1, g] = both.astype(BF16)
                z_copy(g, k).start()

    def d_step(g, carry):
        s = (chunks + g) % RING
        d_copy(g).wait()
        far = jnp.dot(hid[line:], ring[s, :units], preferred_element_type=F32)
        xsend[g] = far.astype(BF16)
        x_copy(g).start()
        yown[g] = jnp.dot(hid[:line], ring[s, :units], preferred_element_type=F32)

        @pl.when(g >= LAG)
        def _():
            pair(g - LAG)
        return carry

    lax.fori_loop(0, groups, d_step, 0)
    for g in range(groups - LAG, groups):
        pair(g)
    for g in range(groups):
        total = fin[g]
        for k in range(1, nz):
            z_copy(g, k).wait_recv()
            total = total + zrecv[k - 1, g].astype(F32)
        out[:, pl.ds(g * 2 * CW, 2 * CW)] = total.astype(BF16)

    for h in range(CUT):
        for b in range(nz):
            cross_copy(b, h, False).wait_send()

            @pl.when((z < nz - 1) & (b <= z))
            def _():
                line_copy(b, h, False, 1, up_send).wait_send()

            @pl.when((z > 0) & (b >= z))
            def _():
                line_copy(b, h, False, -1, dn_send).wait_send()
    for q, (far, c) in enumerate(order):
        if q >= len(order) - KEEP:
            part_copy(q).wait_send()
        hid_copy(q, far, c, gx).wait_send()
    for g in range(groups):
        x_copy(g).wait_send()
        for k in range(1, nz):
            z_copy(g, k).wait_send()


def fused(nz, tokens, gate_weight, up_weight, down_weight):
    rows, depth = tokens.shape
    units, width = down_weight.shape
    line = nz * rows
    chunks, groups = units // CW, width // (2 * CW)
    dma = pltpu.SemaphoreType.DMA
    flops = 2 * 2 * line * units * (2 * depth + width)
    return pl.pallas_call(
        functools.partial(kernel, rows, width, units, nz),
        out_shape=jax.ShapeDtypeStruct((rows, width), BF16),
        in_specs=[pl.BlockSpec(memory_space=pl.ANY)] * 4,
        out_specs=pl.BlockSpec(memory_space=pltpu.VMEM),
        scratch_shapes=[
            pltpu.VMEM((RING, depth, 2 * CW), BF16),
            pltpu.VMEM((2 * line, depth), BF16),
            pltpu.VMEM((2 * line, units), BF16),
            pltpu.VMEM((KEEP, 2, line // 2, 2 * CW), F32),
            pltpu.VMEM((2 * chunks, line // 2, 2 * CW), F32),
            pltpu.VMEM((groups, line, 2 * CW), F32),
            pltpu.VMEM((groups, line, 2 * CW), BF16),
            pltpu.VMEM((groups, line, 2 * CW), BF16),
            pltpu.VMEM((nz - 1, groups, rows, 2 * CW), BF16),
            pltpu.VMEM((nz - 1, groups, rows, 2 * CW), BF16),
            pltpu.VMEM((groups, rows, 2 * CW), F32),
            dma((RING, 2)),
            dma,
            dma((nz, CUT)),
            dma((nz, CUT)),
            dma((nz, CUT)),
            dma((nz, CUT)),
            dma((nz, CUT)),
            dma((KEEP,)),
            dma((2 * chunks,)),
            dma((2 * chunks,)),
            dma((2 * chunks,)),
            dma((groups,)),
            dma((groups,)),
            dma((nz - 1, groups)),
            dma((nz - 1, groups)),
        ],
        compiler_params=pltpu.CompilerParams(
            collective_id=0, has_side_effects=True, vmem_limit_bytes=60 * 2**20
        ),
        cost_estimate=pl.CostEstimate(
            flops=flops, bytes_accessed=2 * units * (2 * depth + width), transcendentals=line * units
        ),
    )(tokens, gate_weight, up_weight, down_weight)


def solution(mesh):
    placed = (P(("groups", "gy"), "gx"), P("gx", "gy"), P("gx", "gy"), P("gy", "gx"))
    gy, gx = mesh.shape["gy"], mesh.shape["gx"]

    def run(tokens, gate_weight, up_weight, down_weight):
        rows, depth = tokens.shape
        units, width = down_weight.shape
        fits = gy == 8 and gx == 2 and rows == 32 and units % CW == 0 and width % (2 * CW) == 0
        fits = fits and units <= depth == width <= 4096
        fits = fits and RING >= width // (2 * CW) and units // CW >= KEEP
        fits = fits and RING <= units // CW and units <= 3328
        if fits:
            return fused(gy // 2, tokens, gate_weight, up_weight, down_weight)
        return local(tokens, gate_weight, up_weight, down_weight)

    return jax.shard_map(
        run, mesh=mesh, in_specs=placed, out_specs=P(("groups", "gy"), "gx"), check_vma=False
    )
```

```python
import functools

import jax
import jax.numpy as jnp
from jax import lax
from jax.experimental import pallas as pl
from jax.experimental.pallas import tpu as pltpu
from jax.sharding import PartitionSpec as P

F32, BF16 = jnp.float32, jnp.bfloat16
MESH = pl.DeviceIdType.MESH
CW = 256
RING = 10
KEEP = 6
BEHIND = 3
LAG = 2
CUT = 4


def local(tokens, gate_weight, up_weight, down_weight):
    piece = lax.all_gather(tokens, "gy", axis=0, tiled=True)
    gate_part = jnp.dot(piece, gate_weight, preferred_element_type=F32)
    up_part = jnp.dot(piece, up_weight, preferred_element_type=F32)
    gate, up = lax.psum((gate_part, up_part), "gx")
    hidden = (jax.nn.silu(gate) * up).astype(BF16)
    summed = lax.psum_scatter(
        jnp.dot(hidden, down_weight, preferred_element_type=F32), "gy", scatter_dimension=0, tiled=True
    )
    return summed.astype(BF16)


def kernel(rows, width, units, nz,
           tok, gw, uw, dw, out,
           ring, x_all, hid, part, precv, yown, xsend, xrecv, zsend, zrecv, fin,
           ring_sem, own_sem, up_send, dn_send, line_recv, xf_send, xf_recv,
           part_send, part_recv, hid_send, hid_recv, xs_send, xs_recv, zs_send, zs_recv):
    gx = lax.axis_index("gx")
    gy = lax.axis_index("gy")
    z, x = gy // 2, gy % 2
    line = nz * rows
    half = line // 2
    chunks, groups = units // CW, width // (2 * CW)
    core = {"gx": 1 - gx}
    across = {"gy": z * 2 + 1 - x}

    def along(zz):
        return {"gy": zz * 2 + x}

    def gu_copy(c, which):
        src = (gw, uw)[which].at[:, pl.ds(pl.multiple_of(c * CW, CW), CW)]
        s = c % RING
        return pltpu.make_async_copy(src, ring.at[s, :, pl.ds(which * CW, CW)], ring_sem.at[s, which])

    def d_copy(g):
        src = dw.at[:, pl.ds(pl.multiple_of(g * 2 * CW, 2 * CW), 2 * CW)]
        s = (chunks + g) % RING
        return pltpu.make_async_copy(src, ring.at[s, pl.ds(0, units)], ring_sem.at[s, 0])

    for c in range(min(RING, chunks)):
        gu_copy(c, 0).start()
        gu_copy(c, 1).start()

    barrier = pltpu.get_barrier_semaphore()
    pl.semaphore_signal(barrier, inc=1, device_id=core, device_id_type=MESH)
    pl.semaphore_signal(barrier, inc=1, device_id=across, device_id_type=MESH)
    for k in range(1, nz):
        pl.semaphore_signal(barrier, inc=1, device_id=along(lax.rem(z + k, nz)), device_id_type=MESH)
    pl.semaphore_wait(barrier, nz + 1)

    cut = tok.shape[1] // CUT

    def place(block, h, far):
        return x_all.at[pl.ds(pl.multiple_of(far * line + block * rows, rows), rows), pl.ds(h * cut, cut)]

    def source(block, h, own):
        return tok.at[:, pl.ds(h * cut, cut)] if own else place(block, h, 0)

    def line_copy(block, h, own, step, sems):
        return pltpu.make_async_remote_copy(
            src_ref=source(block, h, own), dst_ref=place(block, h, 0),
            send_sem=sems.at[block, h], recv_sem=line_recv.at[block, h],
            device_id=along(z + step), device_id_type=MESH)

    def cross_copy(block, h, own):
        return pltpu.make_async_remote_copy(
            src_ref=source(block, h, own), dst_ref=place(block, h, 1),
            send_sem=xf_send.at[block, h], recv_sem=xf_recv.at[block, h],
            device_id=across, device_id_type=MESH)

    for h in range(CUT):
        @pl.when(z < nz - 1)
        def _():
            line_copy(z, h, True, 1, up_send).start()

        @pl.when(z > 0)
        def _():
            line_copy(z, h, True, -1, dn_send).start()

        cross_copy(z, h, True).start()
    keep = pltpu.make_async_copy(tok, x_all.at[pl.ds(pl.multiple_of(z * rows, rows), rows)], own_sem)
    keep.start()
    for t in range(1, nz):
        for h in range(CUT):
            @pl.when(z - t >= 0)
            def _():
                line_copy(z - t, h, False, 1, up_send).wait_recv()

                @pl.when(z < nz - 1)
                def _():
                    line_copy(z - t, h, False, 1, up_send).start()

                cross_copy(z - t, h, False).start()

            @pl.when(z + t < nz)
            def _():
                line_copy(z + t, h, False, -1, dn_send).wait_recv()

                @pl.when(z > 0)
                def _():
                    line_copy(z + t, h, False, -1, dn_send).start()

                cross_copy(z + t, h, False).start()
    keep.wait()

    def part_copy(q):
        return pltpu.make_async_remote_copy(
            src_ref=part.at[q % KEEP, 1 - gx], dst_ref=precv.at[q],
            send_sem=part_send.at[q % KEEP], recv_sem=part_recv.at[q],
            device_id=core, device_id_type=MESH)

    def hid_at(far, c, which):
        at = pl.ds(pl.multiple_of(far * line + which * half, half), half)
        return hid.at[at, pl.ds(pl.multiple_of(c * CW, CW), CW)]

    def hid_copy(q, far, c, which):
        return pltpu.make_async_remote_copy(
            src_ref=hid_at(far, c, which), dst_ref=hid_at(far, c, which),
            send_sem=hid_send.at[q], recv_sem=hid_recv.at[q],
            device_id=core, device_id_type=MESH)

    def step(q, far, c, done):
        @pl.when(q >= KEEP)
        def _():
            part_copy(q - KEEP).wait_send()

        if done is not None:
            part_copy(done[0]).wait_recv()
            both = part[done[0] % KEEP, gx] + precv[done[0]]
            gate, up = both[:, :CW], both[:, CW:]
            hid_at(*done[1:], gx)[...] = (gate / (1.0 + jnp.exp(-gate)) * up).astype(BF16)
        if c is not None:
            term = jnp.dot(x_all[far * line:(far + 1) * line], ring[c % RING], preferred_element_type=F32)
            part[q % KEEP, 0] = term[:half]
            part[q % KEEP, 1] = term[half:]
            part_copy(q).start()
        if done is not None:
            hid_copy(*done, gx).start()

    def arrive(c):
        gu_copy(c, 0).wait()
        gu_copy(c, 1).wait()

    def refill(c):
        nxt = c + RING

        @pl.when(nxt < chunks)
        def _():
            gu_copy(nxt, 0).start()
            gu_copy(nxt, 1).start()

        @pl.when((nxt >= chunks) & (nxt < chunks + groups))
        def _():
            d_copy(nxt - chunks).start()

    def near_step(c, carry):
        arrive(c)
        step(c, 0, c, (c - BEHIND, 0, c - BEHIND))
        return carry

    def far_step(c, carry):
        step(RING + c, 1, c, (RING + c - BEHIND, 1, c - BEHIND))
        refill(c)
        return carry

    order = [(0, c) for c in range(RING)] + [(1, c) for c in range(RING)]
    order += [(far, c) for c in range(RING, chunks) for far in range(2)]

    def before(q):
        return (q - BEHIND,) + order[q - BEHIND]

    for c in range(BEHIND):
        arrive(c)
        step(c, 0, c, None)
    lax.fori_loop(BEHIND, RING, near_step, 0)
    for b in range(nz):
        for h in range(CUT):
            cross_copy(b, h, False).wait_recv()
    for c in range(BEHIND):
        step(RING + c, 1, c, before(RING + c))
        refill(c)
    lax.fori_loop(BEHIND, RING, far_step, 0)
    for c in range(RING, chunks):
        arrive(c)
        step(2 * c, 0, c, before(2 * c))
        step(2 * c + 1, 1, c, before(2 * c + 1))
        refill(c)
    for q in range(2 * chunks, 2 * chunks + BEHIND):
        step(q, 0, None, before(q))
    for q, (far, c) in enumerate(order):
        hid_copy(q, far, c, 1 - gx).wait_recv()

    def x_copy(g):
        return pltpu.make_async_remote_copy(
            src_ref=xsend.at[g], dst_ref=xrecv.at[g], send_sem=xs_send.at[g], recv_sem=xs_recv.at[g],
            device_id=across, device_id_type=MESH)

    def z_copy(g, k):
        return pltpu.make_async_remote_copy(
            src_ref=zsend.at[k - 1, g], dst_ref=zrecv.at[k - 1, g],
            send_sem=zs_send.at[k - 1, g], recv_sem=zs_recv.at[k - 1, g],
            device_id=along(lax.rem(z + k, nz)), device_id_type=MESH)

    def pair(g):
        x_copy(g).wait_recv()
        for k in range(nz):
            at = pl.ds(pl.multiple_of(lax.rem(z + k, nz) * rows, rows), rows)
            both = yown[g, at] + xrecv[g, at].astype(F32)
            if k == 0:
                fin[g] = both
            else:
                zsend[k - 1, g] = both.astype(BF16)
                z_copy(g, k).start()

    def d_step(g, carry):
        s = (chunks + g) % RING
        d_copy(g).wait()
        far = jnp.dot(hid[line:], ring[s, :units], preferred_element_type=F32)
        xsend[g] = far.astype(BF16)
        x_copy(g).start()
        yown[g] = jnp.dot(hid[:line], ring[s, :units], preferred_element_type=F32)

        @pl.when(g >= LAG)
        def _():
            pair(g - LAG)
        return carry

    lax.fori_loop(0, groups, d_step, 0)
    for g in range(groups - LAG, groups):
        pair(g)
    for g in range(groups):
        total = fin[g]
        for k in range(1, nz):
            z_copy(g, k).wait_recv()
            total = total + zrecv[k - 1, g].astype(F32)
        out[:, pl.ds(g * 2 * CW, 2 * CW)] = total.astype(BF16)

    for h in range(CUT):
        for b in range(nz):
            cross_copy(b, h, False).wait_send()

            @pl.when((z < nz - 1) & (b <= z))
            def _():
                line_copy(b, h, False, 1, up_send).wait_send()

            @pl.when((z > 0) & (b >= z))
            def _():
                line_copy(b, h, False, -1, dn_send).wait_send()
    for q, (far, c) in enumerate(order):
        if q >= len(order) + BEHIND - KEEP:
            part_copy(q).wait_send()
        hid_copy(q, far, c, gx).wait_send()
    for g in range(groups):
        x_copy(g).wait_send()
        for k in range(1, nz):
            z_copy(g, k).wait_send()


def fused(nz, tokens, gate_weight, up_weight, down_weight):
    rows, depth = tokens.shape
    units, width = down_weight.shape
    line = nz * rows
    chunks, groups = units // CW, width // (2 * CW)
    dma = pltpu.SemaphoreType.DMA
    flops = 2 * 2 * line * units * (2 * depth + width)
    return pl.pallas_call(
        functools.partial(kernel, rows, width, units, nz),
        out_shape=jax.ShapeDtypeStruct((rows, width), BF16),
        in_specs=[pl.BlockSpec(memory_space=pl.ANY)] * 4,
        out_specs=pl.BlockSpec(memory_space=pltpu.VMEM),
        scratch_shapes=[
            pltpu.VMEM((RING, depth, 2 * CW), BF16),
            pltpu.VMEM((2 * line, depth), BF16),
            pltpu.VMEM((2 * line, units), BF16),
            pltpu.VMEM((KEEP, 2, line // 2, 2 * CW), F32),
            pltpu.VMEM((2 * chunks, line // 2, 2 * CW), F32),
            pltpu.VMEM((groups, line, 2 * CW), F32),
            pltpu.VMEM((groups, line, 2 * CW), BF16),
            pltpu.VMEM((groups, line, 2 * CW), BF16),
            pltpu.VMEM((nz - 1, groups, rows, 2 * CW), BF16),
            pltpu.VMEM((nz - 1, groups, rows, 2 * CW), BF16),
            pltpu.VMEM((groups, rows, 2 * CW), F32),
            dma((RING, 2)),
            dma,
            dma((nz, CUT)),
            dma((nz, CUT)),
            dma((nz, CUT)),
            dma((nz, CUT)),
            dma((nz, CUT)),
            dma((KEEP,)),
            dma((2 * chunks,)),
            dma((2 * chunks,)),
            dma((2 * chunks,)),
            dma((groups,)),
            dma((groups,)),
            dma((nz - 1, groups)),
            dma((nz - 1, groups)),
        ],
        compiler_params=pltpu.CompilerParams(
            collective_id=0, has_side_effects=True, vmem_limit_bytes=60 * 2**20
        ),
        cost_estimate=pl.CostEstimate(
            flops=flops, bytes_accessed=2 * units * (2 * depth + width), transcendentals=line * units
        ),
    )(tokens, gate_weight, up_weight, down_weight)


def solution(mesh):
    placed = (P(("groups", "gy"), "gx"), P("gx", "gy"), P("gx", "gy"), P("gy", "gx"))
    gy, gx = mesh.shape["gy"], mesh.shape["gx"]

    def run(tokens, gate_weight, up_weight, down_weight):
        rows, depth = tokens.shape
        units, width = down_weight.shape
        fits = gy == 8 and gx == 2 and rows == 32 and units % CW == 0 and width % (2 * CW) == 0
        fits = fits and units <= depth == width <= 4096
        fits = fits and RING >= width // (2 * CW) and RING > BEHIND
        fits = fits and RING <= units // CW and units <= 3328
        if fits:
            return fused(gy // 2, tokens, gate_weight, up_weight, down_weight)
        return local(tokens, gate_weight, up_weight, down_weight)

    return jax.shard_map(
        run, mesh=mesh, in_specs=placed, out_specs=P(("groups", "gy"), "gx"), check_vma=False
    )
```
